32 devices in a mesh: ctx: 16 (over z, x, core), tp: 2 (over y).
Axes of the slice: x: 2, y: 2, z: 4, core: 2. Of those that a mesh axis runs over, the one named last changes fastest.
Arguments:
- query_proj: bfloat16 [8192, 4096], P('ctx', 'tp'), may hold values from -6 to 6
- key_proj: bfloat16 [8192, 4096], P('ctx', 'tp'), may hold values from -6 to 6
- value_proj: bfloat16 [8192, 4096], P('ctx', 'tp'), may hold values from -6 to 6
- cotangent: bfloat16 [8192, 4096], P('ctx', 'tp'), may hold values from -6 to 6
- out_weight: bfloat16 [4096, 4096], P('tp'), may hold values from -0.09375 to 0.09375
- decay_rates: float32 [4096, 16], P('tp'), may hold values from 6.1035156e-05 to 0.1
- residues: float32 [4096, 16], P('tp'), may hold values from -1.8 to 1.8
- skip_gain: float32 [4096], P('tp'), may hold values from 0.5 to 1.5
Outputs:
- mixed: bfloat16 [8192, 4096], P('ctx', 'tp')
- grad_query: bfloat16 [8192, 4096], P('ctx', 'tp')
- grad_key: bfloat16 [8192, 4096], P('ctx', 'tp')
- grad_value: bfloat16 [8192, 4096], P('ctx', 'tp')
The draws below stay inside these ranges and needn't reach their ends.
All inputs are finite; a program needn't handle non-finite values.
Results may differ from the reference program's by a relative error of at most 0.023.
Values may be sent and summed in bfloat16 or wider, within the bound.
A program may use at most 128 MiB of HBM per device.

```python
import math
import jax
import jax.numpy as jnp
from jax import lax

D = 4096
STATE = 16
SEQ = 8192
N_TP = 2


def shard_levels(rng, extent, cuts, low, largest):
    gain = 1.0
    for axis_at, parts in cuts:
        steps = jax.random.uniform(jax.random.fold_in(jax.random.fold_in(rng, 6), axis_at), (parts,), jnp.float32, low / len(cuts), largest / len(cuts))
        gain = gain * jnp.repeat(jnp.exp(steps), extent[axis_at] // parts).reshape((-1,) + (1,) * (len(extent) - 1 - axis_at))
    return gain


def normal_values(key, shape, deviation, reach, cuts=(), held_as=jnp.bfloat16):
    values = deviation * jax.random.normal(key, shape, jnp.float32)
    if cuts:
        values = values * shard_levels(key, shape, cuts, -0.22, 0.18)
    return jnp.clip(values, -reach, reach).astype(held_as)


def setup_inputs(seed: int = 0) -> dict:
    keys = jax.random.split(jax.random.key(seed), 9)
    query_proj = normal_values(keys[0], (SEQ, D), 1.0, 6.0, ((0, 16), (1, 2)))
    key_proj = normal_values(keys[1], (SEQ, D), 1.0, 6.0, ((0, 16), (1, 2)))
    value_proj = normal_values(keys[2], (SEQ, D), 1.0, 6.0, ((0, 16), (1, 2)))
    cotangent = normal_values(keys[3], (SEQ, D), 1.0, 6.0, ((0, 16), (1, 2)))
    out_weight = normal_values(keys[4], (D, D), D ** -0.5, 0.09375, ((0, 2),))
    decay_rates = jnp.clip(jnp.exp(math.log(0.1) - 7.4014754 * jax.random.uniform(keys[5], (D, STATE), jnp.float32) ** shard_levels(keys[5], (D, STATE), ((0, 2),), -0.2, 0.2)), 6.103515625e-05, 0.1)
    residues = normal_values(keys[6], (D, STATE), 0.3, 1.8, ((0, 2),), jnp.float32)
    skip_gain = jnp.clip(0.5 + 1.0 * jax.random.uniform(keys[7], (D,), jnp.float32) ** shard_levels(keys[7], (D,), ((0, 2),), -0.2, 0.2), 0.5, 1.5)
    return {"query_proj": query_proj, "key_proj": key_proj, "value_proj": value_proj, "cotangent": cotangent, "out_weight": out_weight, "decay_rates": decay_rates, "residues": residues, "skip_gain": skip_gain}


block_len = 128
highest = lax.Precision.HIGHEST

def pair_combine(earlier, later):
    return (earlier[0] * later[0], earlier[1] * later[0] + later[1])

def amplitude_of(decay_rates, residues):
    return residues * jnp.sqrt(-jnp.expm1(-2.0 * decay_rates))

def toeplitz_table(decay_rates, residues):
    steps_f = jnp.arange(block_len).astype(jnp.float32)
    amplitude = amplitude_of(decay_rates, residues)
    falling = amplitude[:, :, None] * jnp.exp(-decay_rates[:, :, None] * steps_f)
    rising = jnp.exp(decay_rates[:, :, None] * steps_f)
    table = jnp.einsum('cmi,cmj->cij', falling, rising, precision=highest)
    below = steps_f[:, None] >= steps_f[None, :]
    return jnp.where(below[None], table, 0.0)

def tail_table(decay_rates):
    steps_f = jnp.arange(block_len).astype(jnp.float32)
    return jnp.exp(-decay_rates[:, :, None] * (block_len - 1.0 - steps_f))

def head_table(decay_rates, residues):
    steps_f = jnp.arange(block_len).astype(jnp.float32)
    amplitude = amplitude_of(decay_rates, residues)
    return amplitude[:, :, None] * jnp.exp(-decay_rates[:, :, None] * (steps_f + 1.0))

def local_pass(signal, toeplitz, tails, decay_rates):
    channels, length = signal.shape
    blocks = signal.reshape(channels, length // block_len, block_len)
    inside = jnp.einsum('cij,cnj->cni', toeplitz, blocks, precision=highest)
    ends = jnp.einsum('cmj,cnj->nmc', tails, blocks, precision=highest)
    factor = jnp.broadcast_to(jnp.exp(-decay_rates * block_len).T[None], ends.shape)
    _, states = lax.associative_scan(pair_combine, (factor, ends), axis=0)
    return (inside, states)

def grouped_local(signal, decay_rates, residues):
    channels, length = signal.shape
    group_width = math.gcd(64, channels)
    group_count = channels // group_width

    def one_group(operands):
        part_data, part_rates, part_res = operands
        return local_pass(part_data, toeplitz_table(part_rates, part_res), tail_table(part_rates), part_rates)
    inside, states = lax.map(one_group, (signal.reshape(group_count, group_width, length), decay_rates.reshape(group_count, group_width, -1), residues.reshape(group_count, group_width, -1)))
    count = length // block_len
    states = jnp.transpose(states, (1, 2, 0, 3)).reshape(count, states.shape[2], channels)
    return (inside.reshape(channels, count, block_len), states)

def finish(inside, states, initial, heads, decay_rates):
    channels, count, _ = inside.shape
    before = jnp.concatenate([jnp.zeros_like(states[:1]), states[:-1]], axis=0)
    starts = (jnp.arange(count) * block_len).astype(jnp.float32)
    before = before + jnp.exp(-decay_rates.T[None, :, :] * starts[:, None, None]) * initial[None, :, :]
    across = jnp.einsum('cmi,nmc->cni', heads, before, precision=highest)
    return (inside + across).reshape(channels, count * block_len)

def long_conv(signal, decay_rates, residues, flipped):
    data = signal.astype(jnp.float32).T
    if flipped:
        data = data[:, ::-1]
    inside, states = grouped_local(data, decay_rates, residues)
    initial = jnp.zeros_like(states[0])
    result = finish(inside, states, initial, head_table(decay_rates, residues), decay_rates)
    if flipped:
        result = result[:, ::-1]
    return result.astype(jnp.bfloat16).T

def reference(query_proj, key_proj, value_proj, cotangent, out_weight, decay_rates, residues, skip_gain):
    gated = (key_proj.astype(jnp.float32) * value_proj.astype(jnp.float32)).astype(jnp.bfloat16)
    conv_out = long_conv(gated, decay_rates, residues, False)
    summed = conv_out.astype(jnp.float32) + skip_gain[None, :] * gated.astype(jnp.float32)
    output_in = (query_proj.astype(jnp.float32) * summed).astype(jnp.bfloat16)
    shard_cols = D // N_TP
    running = jnp.zeros((SEQ, D), jnp.float32)
    for shard_index in range(N_TP):
        lower = shard_index * shard_cols
        partial_value = jnp.dot(output_in[:, lower:lower + shard_cols], out_weight[lower:lower + shard_cols], preferred_element_type=jnp.float32).astype(jnp.bfloat16)
        running = running + lax.optimization_barrier(partial_value).astype(jnp.float32)
    mixed = running.astype(jnp.bfloat16)
    grad_in = jnp.dot(cotangent, out_weight.T, preferred_element_type=jnp.float32)
    grad_query = (grad_in * summed).astype(jnp.bfloat16)
    grad_conv = (grad_in * query_proj.astype(jnp.float32)).astype(jnp.bfloat16)
    back = long_conv(grad_conv, decay_rates, residues, True)
    grad_gated = back.astype(jnp.float32) + skip_gain[None, :] * grad_conv.astype(jnp.float32)
    grad_key = (grad_gated * value_proj.astype(jnp.float32)).astype(jnp.bfloat16)
    grad_value = (grad_gated * key_proj.astype(jnp.float32)).astype(jnp.bfloat16)
    return (mixed, grad_query, grad_key, grad_value)
```

```python
import functools

import jax
import jax.numpy as jnp
from jax import lax
from jax.experimental import pallas as pl
from jax.experimental.pallas import tpu as pltpu
from jax.sharding import PartitionSpec as P

SEGS = 8
LANES = 128
f32 = jnp.float32
bf16 = jnp.bfloat16
LIMIT = 56 * 1024 * 1024


def tree_sum(terms):
    while len(terms) > 1:
        pairs = [a + b for a, b in zip(terms[0::2], terms[1::2])]
        terms = pairs + ([terms[-1]] if len(terms) % 2 else [])
    return terms[0]


def rows_of(table):
    return [jnp.broadcast_to(table[m : m + 1], (SEGS, LANES)) for m in range(table.shape[0])]


def scan_segments(u_ref, y_ref, rates, amp, states, flipped):
    steps = u_ref.shape[0] // SEGS
    unroll = 8
    lam = rows_of(jnp.exp(-rates))
    gain = None if amp is None else rows_of(amp)

    def body(i, xs):
        for j in range(unroll):
            t = i * unroll + j
            if flipped:
                t = steps - 1 - t
            at = pl.ds(t, SEGS, stride=steps)
            u = u_ref[at, :]
            xs = [l * x + u for l, x in zip(lam, xs)]
            if gain is not None:
                y_ref[at, :] = tree_sum([g * x for g, x in zip(gain, xs)])
        return xs

    return lax.fori_loop(0, steps // unroll, body, states)


def local_ends(u_ref, rates, ends_ref, starts_ref, lanes, flipped):
    steps = u_ref.shape[0] // SEGS
    zero = jnp.zeros((SEGS, LANES), f32)
    ends = scan_segments(u_ref, None, rates, None, [zero] * rates.shape[0], flipped)
    place = lax.broadcasted_iota(jnp.int32, (SEGS, LANES), 0)

    def moved(x, by):
        if flipped:
            return jnp.where(place < SEGS - by, pltpu.roll(x, SEGS - by, 0), 0.0)
        return jnp.where(place >= by, pltpu.roll(x, by, 0), 0.0)

    factors = []
    by = 1
    while by < SEGS:
        factors.append((by, rows_of(jnp.exp(-rates * float(steps * by)))))
        by *= 2
    last = 0 if flipped else SEGS - 1
    for m, x in enumerate(ends):
        for by, factor in factors:
            x = x + factor[m] * moved(x, by)
        ends_ref[m : m + 1, lanes] = x[last : last + 1]
        starts_ref[m * SEGS : (m + 1) * SEGS, lanes] = moved(x, 1)


def full_scan(u_ref, y_ref, rates, amp, starts_ref, init, lanes, flipped):
    steps = u_ref.shape[0] // SEGS
    place = lax.broadcasted_iota(jnp.int32, (SEGS, LANES), 0)
    if flipped:
        place = SEGS - 1 - place
    past = place.astype(f32) * float(steps)
    states = []
    for m in range(rates.shape[0]):
        factor = jnp.exp(-rates[m : m + 1] * past)
        states.append(starts_ref[m * SEGS : (m + 1) * SEGS, lanes] + factor * init[m : m + 1])
    scan_segments(u_ref, y_ref, rates, amp, states, flipped)


def lane_groups(width):
    return [slice(g * LANES, (g + 1) * LANES) for g in range(width // LANES)]


def forward_ends_kernel(k_ref, v_ref, rates_ref, ends_ref, starts_ref, u_ref):
    for lanes in lane_groups(k_ref.shape[1]):
        gated = k_ref[:, lanes].astype(f32) * v_ref[:, lanes].astype(f32)
        u_ref[...] = gated.astype(bf16).astype(f32)
        local_ends(u_ref, rates_ref[:, lanes], ends_ref, starts_ref, lanes, False)


def forward_kernel(
    q_ref, k_ref, v_ref, rates_ref, amp_ref, skip_ref, starts_ref, init_ref,
    out_ref, summed_ref, u_ref, y_ref,
):
    for lanes in lane_groups(k_ref.shape[1]):
        gated = k_ref[:, lanes].astype(f32) * v_ref[:, lanes].astype(f32)
        u_ref[...] = gated.astype(bf16).astype(f32)
        full_scan(
            u_ref, y_ref, rates_ref[:, lanes], amp_ref[:, lanes], starts_ref,
            init_ref[:, lanes], lanes, False,
        )
        conv = y_ref[...].astype(bf16).astype(f32)
        summed = conv + skip_ref[:, lanes] * u_ref[...]
        summed_ref[:, lanes] = summed.astype(bf16)
        out_ref[:, lanes] = (q_ref[:, lanes].astype(f32) * summed).astype(bf16)


def matmul_kernel(at_ref, x_ref, w_ref, out_ref):
    out_ref[...] = jnp.dot(x_ref[...], w_ref[...], preferred_element_type=f32).astype(bf16)


def grad_kernel(n_tp, at_ref, *refs):
    cots, weights = refs[:n_tp], refs[n_tp : 2 * n_tp]
    q_ref, summed_ref, rates_ref = refs[2 * n_tp : 2 * n_tp + 3]
    grad_query_ref, grad_conv_ref, ends_ref, starts_ref, u_ref = refs[2 * n_tp + 3 :]
    grad_in = sum(
        lax.dot_general(
            c_ref[...], w_ref[...], (((1,), (1,)), ((), ())), preferred_element_type=f32
        )
        for c_ref, w_ref in zip(cots, weights)
    )
    grad_query_ref[...] = (grad_in * summed_ref[...].astype(f32)).astype(bf16)
    grad_conv_ref[...] = (grad_in * q_ref[...].astype(f32)).astype(bf16)
    for lanes in lane_groups(q_ref.shape[1]):
        u_ref[...] = grad_conv_ref[:, lanes].astype(f32)
        local_ends(u_ref, rates_ref[:, lanes], ends_ref, starts_ref, lanes, True)


def backward_kernel(
    g_ref, k_ref, v_ref, rates_ref, amp_ref, skip_ref, starts_ref, init_ref,
    grad_key_ref, grad_value_ref, u_ref, y_ref,
):
    for lanes in lane_groups(k_ref.shape[1]):
        u_ref[...] = g_ref[:, lanes].astype(f32)
        full_scan(
            u_ref, y_ref, rates_ref[:, lanes], amp_ref[:, lanes], starts_ref,
            init_ref[:, lanes], lanes, True,
        )
        back = y_ref[...].astype(bf16).astype(f32)
        grad = back + skip_ref[:, lanes] * u_ref[...]
        grad_key_ref[:, lanes] = (grad * v_ref[:, lanes].astype(f32)).astype(bf16)
        grad_value_ref[:, lanes] = (grad * k_ref[:, lanes].astype(f32)).astype(bf16)


def across_devices(ends, rates, length, flipped):
    count = lax.axis_size("ctx")
    modes, channels = ends.shape
    rows = modes * channels // LANES

    def spread(x):
        return x.reshape(modes, channels // LANES, LANES).reshape(rows, LANES)

    mine = lax.all_to_all(
        spread(ends).reshape(count, rows // count, LANES), "ctx", split_axis=0, concat_axis=0
    )
    width = rows // count
    my_rates = lax.dynamic_slice_in_dim(spread(rates), lax.axis_index("ctx") * width, width, 0)
    factor = jnp.exp(-my_rates * float(length))
    state = jnp.zeros_like(mine[0])
    before = [None] * count
    for place in reversed(range(count)) if flipped else range(count):
        before[place] = state
        state = factor * state + mine[place]
    back = lax.all_to_all(jnp.stack(before), "ctx", split_axis=0, concat_axis=0)
    return back.reshape(modes, channels)


def per_device(q, k, v, cot, weight, decay_rates, residues, skip_gain):
    length, channels = q.shape
    modes = decay_rates.shape[1]
    n_tp = lax.axis_size("tp")
    me = lax.axis_index("tp").astype(jnp.int32)
    shared = cot.shape[1]

    others = [
        lax.ppermute(cot, "tp", [((i + s) % n_tp, i) for i in range(n_tp)])
        for s in range(1, n_tp)
    ]

    rates = decay_rates.T
    amp = (residues * jnp.sqrt(-jnp.expm1(-2.0 * decay_rates))).T
    skip = skip_gain.reshape(1, channels)

    block = 256
    steps = channels // block
    wide = pl.BlockSpec((length, block), lambda i: (0, i))
    table = pl.BlockSpec((modes, block), lambda i: (0, i))
    starts_spec = pl.BlockSpec((modes * SEGS, block), lambda i: (0, i))
    line = pl.BlockSpec((1, block), lambda i: (0, i))
    params = pltpu.CompilerParams(vmem_limit_bytes=LIMIT)
    signal = jax.ShapeDtypeStruct((length, channels), bf16)
    ends_shape = jax.ShapeDtypeStruct((modes, channels), f32)
    starts_shape = jax.ShapeDtypeStruct((modes * SEGS, channels), f32)
    scratch = pltpu.VMEM((length, LANES), f32)
    cell = length * channels * modes

    ends, starts = pl.pallas_call(
        forward_ends_kernel,
        grid=(steps,),
        in_specs=[wide, wide, table],
        out_specs=[table, starts_spec],
        out_shape=[ends_shape, starts_shape],
        scratch_shapes=[scratch],
        compiler_params=params,
        cost_estimate=pl.CostEstimate(
            flops=2 * cell, bytes_accessed=length * channels * 6, transcendentals=0
        ),
        name="forward_ends",
    )(k, v, rates)
    init = across_devices(ends, rates, length, False)
    output_in, summed = pl.pallas_call(
        forward_kernel,
        grid=(steps,),
        in_specs=[wide, wide, wide, table, table, line, starts_spec, table],
        out_specs=[wide, wide],
        out_shape=[signal, signal],
        scratch_shapes=[scratch, scratch],
        compiler_params=params,
        cost_estimate=pl.CostEstimate(
            flops=4 * cell, bytes_accessed=length * channels * 12, transcendentals=0
        ),
        name="forward_scan",
    )(q, k, v, rates, amp, skip, starts, init)

    cols = 512
    per_target = shared // cols

    def project(target):
        return pl.pallas_call(
            matmul_kernel,
            grid_spec=pltpu.PrefetchScalarGridSpec(
                num_scalar_prefetch=1,
                grid=(per_target,),
                in_specs=[
                    pl.BlockSpec((length, channels), lambda i, at: (0, 0)),
                    pl.BlockSpec((channels, cols), lambda i, at: (0, at[0] * per_target + i)),
                ],
                out_specs=pl.BlockSpec((length, cols), lambda i, at: (0, i)),
            ),
            out_shape=jax.ShapeDtypeStruct((length, shared), bf16),
            compiler_params=params,
            cost_estimate=pl.CostEstimate(
                flops=2 * length * channels * shared,
                bytes_accessed=2 * (channels * shared + length * (channels + shared)),
                transcendentals=0,
            ),
            name="project",
        )(target.reshape(1), output_in, weight)

    received = [
        lax.ppermute(
            project(lax.rem(me + s, n_tp)), "tp", [(i, (i + s) % n_tp) for i in range(n_tp)]
        )
        for s in range(1, n_tp)
    ]

    def weight_spec(s):
        return pl.BlockSpec((block, shared), lambda i, at: (i, lax.rem(at[0] + s, n_tp)))

    def with_at(spec):
        return pl.BlockSpec(spec.block_shape, lambda i, at: (0, i))

    grad_query, grad_conv, back_ends, back_starts = pl.pallas_call(
        functools.partial(grad_kernel, n_tp),
        grid_spec=pltpu.PrefetchScalarGridSpec(
            num_scalar_prefetch=1,
            grid=(steps,),
            in_specs=[pl.BlockSpec((length, shared), lambda i, at: (0, 0))] * n_tp
            + [weight_spec(s) for s in range(n_tp)]
            + [with_at(wide), with_at(wide), with_at(table)],
            out_specs=[with_at(wide), with_at(wide), with_at(table), with_at(starts_spec)],
            scratch_shapes=[scratch],
        ),
        out_shape=[signal, signal, ends_shape, starts_shape],
        compiler_params=params,
        cost_estimate=pl.CostEstimate(
            flops=2 * length * channels * shared * n_tp,
            bytes_accessed=2 * n_tp * shared * channels + length * channels * 8,
            transcendentals=0,
        ),
        name="grad_projection",
    )(me.reshape(1), cot, *others, *([weight] * n_tp), q, summed, rates)
    own = project(me)
    back_init = across_devices(back_ends, rates, length, True)
    grad_key, grad_value = pl.pallas_call(
        backward_kernel,
        grid=(steps,),
        in_specs=[wide, wide, wide, table, table, line, starts_spec, table],
        out_specs=[wide, wide],
        out_shape=[signal, signal],
        scratch_shapes=[scratch, scratch],
        compiler_params=params,
        cost_estimate=pl.CostEstimate(
            flops=4 * cell, bytes_accessed=length * channels * 12, transcendentals=0
        ),
        name="backward_scan",
    )(grad_conv, k, v, rates, amp, skip, back_starts, back_init)

    mixed = own.astype(f32)
    for part in received:
        mixed = mixed + part.astype(f32)
    return (mixed.astype(bf16), grad_query, grad_key, grad_value)


def solution(mesh):
    spread = P("ctx", "tp")
    by_tp = P("tp", None)
    return jax.shard_map(
        per_device,
        mesh=mesh,
        in_specs=(spread, spread, spread, spread, by_tp, by_tp, by_tp, P("tp")),
        out_specs=(spread, spread, spread, spread),
        check_vma=False,
    )
```

```python
import functools

import jax
import jax.numpy as jnp
from jax import lax
from jax.experimental import pallas as pl
from jax.experimental.pallas import tpu as pltpu
from jax.sharding import PartitionSpec as P

SEGS = 8
LANES = 128
GAP = 8
f32 = jnp.float32
bf16 = jnp.bfloat16
LIMIT = 56 * 1024 * 1024
LIGHT = pl.CostEstimate(flops=0, bytes_accessed=0, transcendentals=0)


def tree_sum(terms):
    while len(terms) > 1:
        pairs = [a + b for a, b in zip(terms[0::2], terms[1::2])]
        terms = pairs + ([terms[-1]] if len(terms) % 2 else [])
    return terms[0]


def rows_of(table):
    return [jnp.broadcast_to(table[m : m + 1], (SEGS, LANES)) for m in range(table.shape[0])]


def put_segments(ref, value):
    steps = value.shape[0] // SEGS
    for s in range(SEGS):
        ref[s * (steps + GAP) : s * (steps + GAP) + steps] = value[s * steps : (s + 1) * steps]


def get_segments(ref):
    steps = ref.shape[0] // SEGS - GAP
    return jnp.concatenate(
        [ref[s * (steps + GAP) : s * (steps + GAP) + steps] for s in range(SEGS)], axis=0
    )


def step_rows(steps, t, flipped):
    return pl.ds(steps - 1 - t if flipped else t, SEGS, stride=steps + GAP)


def scan_ends(u_ref, rates, flipped):
    steps = u_ref.shape[0] // SEGS - GAP
    half = steps // 2
    unroll = 8
    lam = rows_of(jnp.exp(-rates))

    def body(i, carry):
        early, late = carry
        for j in range(unroll):
            t = i * unroll + j
            u = u_ref[step_rows(steps, t, flipped), :]
            w = u_ref[step_rows(steps, t + half, flipped), :]
            early = [l * x + u for l, x in zip(lam, early)]
            late = [l * x + w for l, x in zip(lam, late)]
        return early, late

    zero = [jnp.zeros((SEGS, LANES), f32)] * rates.shape[0]
    early, late = lax.fori_loop(0, half // unroll, body, (zero, zero))
    factor = rows_of(jnp.exp(-rates * float(half)))
    return [f * x + y for f, x, y in zip(factor, early, late)]


def scan_signal(u_ref, y_ref, rates, amp, states, flipped):
    steps = u_ref.shape[0] // SEGS - GAP
    unroll = 8
    lam = rows_of(jnp.exp(-rates))
    gain = rows_of(amp)

    def body(i, xs):
        for j in range(unroll):
            at = step_rows(steps, i * unroll + j, flipped)
            u = u_ref[at, :]
            xs = [l * x + u for l, x in zip(lam, xs)]
            y_ref[at, :] = tree_sum([g * x for g, x in zip(gain, xs)])
        return xs

    lax.fori_loop(0, steps // unroll, body, states)


def local_ends(u_ref, rates, ends_ref, starts_ref, lanes, rows, flipped):
    steps = u_ref.shape[0] // SEGS - GAP
    ends = scan_ends(u_ref, rates, flipped)
    place = lax.broadcasted_iota(jnp.int32, (SEGS, LANES), 0)

    def moved(x, by):
        if flipped:
            return jnp.where(place < SEGS - by, pltpu.roll(x, SEGS - by, 0), 0.0)
        return jnp.where(place >= by, pltpu.roll(x, by, 0), 0.0)

    factors = []
    by = 1
    while by < SEGS:
        factors.append((by, rows_of(jnp.exp(-rates * float(steps * by)))))
        by *= 2
    last = 0 if flipped else SEGS - 1
    for m, x in enumerate(ends):
        for by, factor in factors:
            x = x + factor[m] * moved(x, by)
        ends_ref[rows.start + m : rows.start + m + 1] = x[last : last + 1]
        starts_ref[m * SEGS : (m + 1) * SEGS, lanes] = moved(x, 1)


def full_scan(u_ref, y_ref, rates, amp, starts_ref, init, lanes, flipped):
    steps = u_ref.shape[0] // SEGS - GAP
    place = lax.broadcasted_iota(jnp.int32, (SEGS, LANES), 0)
    if flipped:
        place = SEGS - 1 - place
    past = place.astype(f32) * float(steps)
    states = []
    for m in range(rates.shape[0]):
        factor = jnp.exp(-rates[m : m + 1] * past)
        states.append(starts_ref[m * SEGS : (m + 1) * SEGS, lanes] + factor * init[m : m + 1])
    scan_signal(u_ref, y_ref, rates, amp, states, flipped)


def lane_groups(width, modes):
    return [
        (slice(g * LANES, (g + 1) * LANES), slice(g * modes, (g + 1) * modes))
        for g in range(width // LANES)
    ]


def groups_of(signal_ref, table_ref):
    width = signal_ref.shape[1]
    return lane_groups(width, table_ref.shape[0] * LANES // width)


def forward_ends_kernel(k_ref, v_ref, rates_ref, ends_ref, starts_ref, u_ref):
    for lanes, rows in groups_of(k_ref, rates_ref):
        gated = k_ref[:, lanes].astype(f32) * v_ref[:, lanes].astype(f32)
        gated = gated.astype(bf16).astype(f32)
        put_segments(u_ref, gated)
        local_ends(u_ref, rates_ref[rows], ends_ref, starts_ref, lanes, rows, False)


def forward_kernel(
    q_ref, k_ref, v_ref, rates_ref, amp_ref, skip_ref, starts_ref, init_ref,
    out_ref, summed_ref, u_ref, y_ref,
):
    for lanes, rows in groups_of(k_ref, rates_ref):
        gated = k_ref[:, lanes].astype(f32) * v_ref[:, lanes].astype(f32)
        gated = gated.astype(bf16).astype(f32)
        put_segments(u_ref, gated)
        full_scan(
            u_ref, y_ref, rates_ref[rows], amp_ref[rows], starts_ref,
            init_ref[rows], lanes, False,
        )
        conv = get_segments(y_ref).astype(bf16).astype(f32)
        summed = conv + skip_ref[:, lanes] * get_segments(u_ref)
        summed_ref[:, lanes] = summed.astype(bf16)
        out_ref[:, lanes] = (q_ref[:, lanes].astype(f32) * summed).astype(bf16)


def matmul_kernel(at_ref, x_ref, w_ref, out_ref):
    out_ref[...] = jnp.dot(x_ref[...], w_ref[...], preferred_element_type=f32).astype(bf16)


def grad_kernel(n_tp, at_ref, *refs):
    cots, weights = refs[:n_tp], refs[n_tp : 2 * n_tp]
    q_ref, summed_ref, rates_ref = refs[2 * n_tp : 2 * n_tp + 3]
    grad_query_ref, grad_conv_ref, ends_ref, starts_ref, u_ref = refs[2 * n_tp + 3 :]
    grad_in = sum(
        lax.dot_general(
            c_ref[...], w_ref[...], (((1,), (1,)), ((), ())), preferred_element_type=f32
        )
        for c_ref, w_ref in zip(cots, weights)
    )
    grad_query_ref[...] = (grad_in * summed_ref[...].astype(f32)).astype(bf16)
    grad_conv_ref[...] = (grad_in * q_ref[...].astype(f32)).astype(bf16)
    for lanes, rows in groups_of(q_ref, rates_ref):
        put_segments(u_ref, grad_conv_ref[:, lanes].astype(f32))
        local_ends(u_ref, rates_ref[rows], ends_ref, starts_ref, lanes, rows, True)


def backward_kernel(
    g_ref, k_ref, v_ref, rates_ref, amp_ref, skip_ref, starts_ref, init_ref,
    grad_key_ref, grad_value_ref, u_ref, y_ref,
):
    for lanes, rows in groups_of(k_ref, rates_ref):
        put_segments(u_ref, g_ref[:, lanes].astype(f32))
        full_scan(
            u_ref, y_ref, rates_ref[rows], amp_ref[rows], starts_ref,
            init_ref[rows], lanes, True,
        )
        back = get_segments(y_ref).astype(bf16).astype(f32)
        grad = back + skip_ref[:, lanes] * get_segments(u_ref)
        grad_key_ref[:, lanes] = (grad * v_ref[:, lanes].astype(f32)).astype(bf16)
        grad_value_ref[:, lanes] = (grad * k_ref[:, lanes].astype(f32)).astype(bf16)


def exchange_kernel(
    length, flipped, ends_ref, rates_ref, init_ref,
    mine_ref, before_ref, back_ref, send_out, recv_out, send_back, recv_back,
):
    count = ends_ref.shape[0]
    me, row = lax.axis_index("ctx"), lax.axis_index("tp")
    partners = [lax.rem(me + p, count) for p in range(1, count)]

    barrier = pltpu.get_barrier_semaphore()
    for to in partners:
        pl.semaphore_signal(
            barrier, inc=1, device_id=(to, row), device_id_type=pl.DeviceIdType.MESH
        )
    pl.semaphore_wait(barrier, count - 1)

    def send(src_ref, dst_ref, sent, arrived):
        copies = [
            pltpu.make_async_remote_copy(
                src_ref=src_ref.at[to],
                dst_ref=dst_ref.at[me],
                send_sem=sent.at[p],
                recv_sem=arrived.at[p],
                device_id=(to, row),
                device_id_type=pl.DeviceIdType.MESH,
            )
            for p, to in enumerate(partners)
        ]
        for copy in copies:
            copy.start()
        return copies

    outward = send(ends_ref, mine_ref, send_out, recv_out)
    mine_ref[me] = ends_ref[me]
    factor = jnp.exp(-rates_ref[me] * float(length))
    for copy in outward:
        copy.wait_recv()
    state = jnp.zeros_like(factor)
    for place in reversed(range(count)) if flipped else range(count):
        before_ref[place] = state
        state = factor * state + mine_ref[place]
    homeward = send(before_ref, back_ref, send_back, recv_back)
    back_ref[me] = before_ref[me]
    for copy in homeward:
        copy.wait_recv()
    init_ref[...] = back_ref[...]
    for copy in outward + homeward:
        copy.wait_send()


def across_devices(ends, rates, length, flipped):
    count = lax.axis_size("ctx")
    rows = ends.shape[0]
    shape = (count, rows // count, LANES)
    whole = pl.BlockSpec(memory_space=pltpu.VMEM)
    init = pl.pallas_call(
        functools.partial(exchange_kernel, length, flipped),
        out_shape=jax.ShapeDtypeStruct(shape, f32),
        in_specs=[whole, whole],
        out_specs=whole,
        scratch_shapes=[pltpu.VMEM(shape, f32)] * 3
        + [pltpu.SemaphoreType.DMA((count - 1,))] * 4,
        compiler_params=pltpu.CompilerParams(
            collective_id=1 if flipped else 0, has_side_effects=True
        ),
        cost_estimate=LIGHT,
        name="exchange_back" if flipped else "exchange_forward",
    )(ends.reshape(shape), rates.reshape(shape))
    return init.reshape(rows, LANES)


def per_device(q, k, v, cot, weight, decay_rates, residues, skip_gain):
    length, channels = q.shape
    modes = decay_rates.shape[1]
    n_tp = lax.axis_size("tp")
    me = lax.axis_index("tp").astype(jnp.int32)
    shared = cot.shape[1]

    others = [
        lax.ppermute(cot, "tp", [((i + s) % n_tp, i) for i in range(n_tp)])
        for s in range(1, n_tp)
    ]

    def by_group(x):
        x = jnp.transpose(x.reshape(channels // LANES, LANES, modes), (0, 2, 1))
        return x.reshape(channels // LANES * modes, LANES)

    rates = by_group(decay_rates)
    amp = by_group(residues * jnp.sqrt(-jnp.expm1(-2.0 * decay_rates)))
    skip = skip_gain.reshape(1, channels)

    block = 256
    steps = channels // block
    wide = pl.BlockSpec((length, block), lambda i: (0, i))
    table = pl.BlockSpec((block // LANES * modes, LANES), lambda i: (i, 0))
    starts_spec = pl.BlockSpec((modes * SEGS, block), lambda i: (0, i))
    line = pl.BlockSpec((1, block), lambda i: (0, i))
    params = pltpu.CompilerParams(vmem_limit_bytes=LIMIT)
    signal = jax.ShapeDtypeStruct((length, channels), bf16)
    ends_shape = jax.ShapeDtypeStruct((channels // LANES * modes, LANES), f32)
    starts_shape = jax.ShapeDtypeStruct((modes * SEGS, channels), f32)
    scratch = pltpu.VMEM((length + SEGS * GAP, LANES), f32)

    ends, starts = pl.pallas_call(
        forward_ends_kernel,
        grid=(steps,),
        in_specs=[wide, wide, table],
        out_specs=[table, starts_spec],
        out_shape=[ends_shape, starts_shape],
        scratch_shapes=[scratch],
        compiler_params=params,
        cost_estimate=LIGHT,
        name="forward_ends",
    )(k, v, rates)
    init = across_devices(ends, rates, length, False)
    output_in, summed = pl.pallas_call(
        forward_kernel,
        grid=(steps,),
        in_specs=[wide, wide, wide, table, table, line, starts_spec, table],
        out_specs=[wide, wide],
        out_shape=[signal, signal],
        scratch_shapes=[scratch, scratch],
        compiler_params=params,
        cost_estimate=LIGHT,
        name="forward_scan",
    )(q, k, v, rates, amp, skip, starts, init)

    cols = 512
    per_target = shared // cols

    def project(target):
        return pl.pallas_call(
            matmul_kernel,
            grid_spec=pltpu.PrefetchScalarGridSpec(
                num_scalar_prefetch=1,
                grid=(per_target,),
                in_specs=[
                    pl.BlockSpec((length, channels), lambda i, at: (0, 0)),
                    pl.BlockSpec((channels, cols), lambda i, at: (0, at[0] * per_target + i)),
                ],
                out_specs=pl.BlockSpec((length, cols), lambda i, at: (0, i)),
            ),
            out_shape=jax.ShapeDtypeStruct((length, shared), bf16),
            compiler_params=params,
            cost_estimate=LIGHT,
            name="project",
        )(target.reshape(1), output_in, weight)

    parts = [project(lax.rem(me + s, n_tp)) for s in range(1, n_tp)]
    others, parts = lax.optimization_barrier((others, parts))
    received = [
        lax.ppermute(part, "tp", [(i, (i + s) % n_tp) for i in range(n_tp)])
        for s, part in enumerate(parts, 1)
    ]

    def weight_spec(s):
        return pl.BlockSpec((block, shared), lambda i, at: (i, lax.rem(at[0] + s, n_tp)))

    def with_at(spec):
        return pl.BlockSpec(spec.block_shape, lambda i, at: spec.index_map(i))

    grad_query, grad_conv, back_ends, back_starts = pl.pallas_call(
        functools.partial(grad_kernel, n_tp),
        grid_spec=pltpu.PrefetchScalarGridSpec(
            num_scalar_prefetch=1,
            grid=(steps,),
            in_specs=[pl.BlockSpec((length, shared), lambda i, at: (0, 0))] * n_tp
            + [weight_spec(s) for s in range(n_tp)]
            + [with_at(wide), with_at(wide), with_at(table)],
            out_specs=[with_at(wide), with_at(wide), with_at(table), with_at(starts_spec)],
            scratch_shapes=[scratch],
        ),
        out_shape=[signal, signal, ends_shape, starts_shape],
        compiler_params=params,
        cost_estimate=LIGHT,
        name="grad_projection",
    )(me.reshape(1), cot, *others, *([weight] * n_tp), q, summed, rates)
    own = project(me)
    back_init = across_devices(back_ends, rates, length, True)
    grad_key, grad_value = pl.pallas_call(
        backward_kernel,
        grid=(steps,),
        in_specs=[wide, wide, wide, table, table, line, starts_spec, table],
        out_specs=[wide, wide],
        out_shape=[signal, signal],
        scratch_shapes=[scratch, scratch],
        compiler_params=params,
        cost_estimate=LIGHT,
        name="backward_scan",
    )(grad_conv, k, v, rates, amp, skip, back_starts, back_init)

    mixed = own.astype(f32)
    for part in received:
        mixed = mixed + part.astype(f32)
    return (mixed.astype(bf16), grad_query, grad_key, grad_value)


def solution(mesh):
    spread = P("ctx", "tp")
    by_tp = P("tp", None)
    return jax.shard_map(
        per_device,
        mesh=mesh,
        in_specs=(spread, spread, spread, spread, by_tp, by_tp, by_tp, P("tp")),
        out_specs=(spread, spread, spread, spread),
        check_vma=False,
    )
```

```python
import functools

import jax
import jax.numpy as jnp
from jax import lax
from jax.experimental import pallas as pl
from jax.experimental.pallas import tpu as pltpu
from jax.sharding import PartitionSpec as P

SEGS = 8
LANES = 128
GAP = 8
f32 = jnp.float32
bf16 = jnp.bfloat16
LIMIT = 56 * 1024 * 1024
LIGHT = pl.CostEstimate(flops=0, bytes_accessed=0, transcendentals=0)


def tree_sum(terms):
    while len(terms) > 1:
        pairs = [a + b for a, b in zip(terms[0::2], terms[1::2])]
        terms = pairs + ([terms[-1]] if len(terms) % 2 else [])
    return terms[0]


def rows_of(table):
    return [jnp.broadcast_to(table[m : m + 1], (SEGS, LANES)) for m in range(table.shape[0])]


def put_segments(ref, value):
    steps = value.shape[0] // SEGS
    for s in range(SEGS):
        ref[s * (steps + GAP) : s * (steps + GAP) + steps] = value[s * steps : (s + 1) * steps]


def get_segments(ref):
    steps = ref.shape[0] // SEGS - GAP
    return jnp.concatenate(
        [ref[s * (steps + GAP) : s * (steps + GAP) + steps] for s in range(SEGS)], axis=0
    )


def step_rows(steps, t, flipped):
    return pl.ds(steps - 1 - t if flipped else t, SEGS, stride=steps + GAP)


def scan_ends(u_ref, rates, flipped):
    steps = u_ref.shape[0] // SEGS - GAP
    half = steps // 2
    unroll = 8
    lam = rows_of(jnp.exp(-rates))

    def body(i, carry):
        early, late = carry
        for j in range(unroll):
            t = i * unroll + j
            u = u_ref[step_rows(steps, t, flipped), :]
            w = u_ref[step_rows(steps, t + half, flipped), :]
            early = [l * x + u for l, x in zip(lam, early)]
            late = [l * x + w for l, x in zip(lam, late)]
        return early, late

    zero = [jnp.zeros((SEGS, LANES), f32)] * rates.shape[0]
    early, late = lax.fori_loop(0, half // unroll, body, (zero, zero))
    factor = rows_of(jnp.exp(-rates * float(half)))
    return [f * x + y for f, x, y in zip(factor, early, late)]


def scan_signal(u_ref, y_ref, rates, amp, states, flipped):
    steps = u_ref.shape[0] // SEGS - GAP
    unroll = 8
    lam = rows_of(jnp.exp(-rates))
    gain = rows_of(amp)

    def body(i, xs):
        for j in range(unroll):
            at = step_rows(steps, i * unroll + j, flipped)
            u = u_ref[at, :]
            xs = [l * x + u for l, x in zip(lam, xs)]
            y_ref[at, :] = tree_sum([g * x for g, x in zip(gain, xs)])
        return xs

    lax.fori_loop(0, steps // unroll, body, states)


def local_ends(u_ref, rates, ends_ref, starts_ref, lanes, rows, flipped):
    steps = u_ref.shape[0] // SEGS - GAP
    ends = scan_ends(u_ref, rates, flipped)
    place = lax.broadcasted_iota(jnp.int32, (SEGS, LANES), 0)

    def moved(x, by):
        if flipped:
            return jnp.where(place < SEGS - by, pltpu.roll(x, SEGS - by, 0), 0.0)
        return jnp.where(place >= by, pltpu.roll(x, by, 0), 0.0)

    factors = []
    by = 1
    while by < SEGS:
        factors.append((by, rows_of(jnp.exp(-rates * float(steps * by)))))
        by *= 2
    last = 0 if flipped else SEGS - 1
    for m, x in enumerate(ends):
        for by, factor in factors:
            x = x + factor[m] * moved(x, by)
        ends_ref[rows.start + m : rows.start + m + 1] = x[last : last + 1]
        starts_ref[m * SEGS : (m + 1) * SEGS, lanes] = moved(x, 1)


def full_scan(u_ref, y_ref, rates, amp, starts_ref, init, lanes, flipped):
    steps = u_ref.shape[0] // SEGS - GAP
    place = lax.broadcasted_iota(jnp.int32, (SEGS, LANES), 0)
    if flipped:
        place = SEGS - 1 - place
    past = place.astype(f32) * float(steps)
    states = []
    for m in range(rates.shape[0]):
        factor = jnp.exp(-rates[m : m + 1] * past)
        states.append(starts_ref[m * SEGS : (m + 1) * SEGS, lanes] + factor * init[m : m + 1])
    scan_signal(u_ref, y_ref, rates, amp, states, flipped)


def lane_groups(width, modes):
    return [
        (slice(g * LANES, (g + 1) * LANES), slice(g * modes, (g + 1) * modes))
        for g in range(width // LANES)
    ]


def groups_of(signal_ref, table_ref):
    width = signal_ref.shape[1]
    return lane_groups(width, table_ref.shape[0] * LANES // width)


def forward_ends_kernel(k_ref, v_ref, rates_ref, ends_ref, starts_ref, u_ref):
    for lanes, rows in groups_of(k_ref, rates_ref):
        gated = k_ref[:, lanes].astype(f32) * v_ref[:, lanes].astype(f32)
        gated = gated.astype(bf16).astype(f32)
        put_segments(u_ref, gated)
        local_ends(u_ref, rates_ref[rows], ends_ref, starts_ref, lanes, rows, False)


def forward_kernel(
    q_ref, k_ref, v_ref, rates_ref, amp_ref, skip_ref, starts_ref, init_ref,
    out_ref, summed_ref, u_ref, y_ref,
):
    for lanes, rows in groups_of(k_ref, rates_ref):
        gated = k_ref[:, lanes].astype(f32) * v_ref[:, lanes].astype(f32)
        gated = gated.astype(bf16).astype(f32)
        put_segments(u_ref, gated)
        full_scan(
            u_ref, y_ref, rates_ref[rows], amp_ref[rows], starts_ref,
            init_ref[rows], lanes, False,
        )
        conv = get_segments(y_ref).astype(bf16).astype(f32)
        summed = conv + skip_ref[:, lanes] * get_segments(u_ref)
        summed_ref[:, lanes] = summed.astype(bf16)
        out_ref[:, lanes] = (q_ref[:, lanes].astype(f32) * summed).astype(bf16)


def matmul_kernel(at_ref, x_ref, w_ref, out_ref):
    out_ref[...] = jnp.dot(x_ref[...], w_ref[...], preferred_element_type=f32).astype(bf16)


def grad_kernel(n_tp, at_ref, *refs):
    cots, weights = refs[:n_tp], refs[n_tp : 2 * n_tp]
    q_ref, summed_ref, rates_ref = refs[2 * n_tp : 2 * n_tp + 3]
    grad_query_ref, grad_conv_ref, ends_ref, starts_ref, u_ref = refs[2 * n_tp + 3 :]
    grad_in = sum(
        lax.dot_general(
            c_ref[...], w_ref[...], (((1,), (1,)), ((), ())), preferred_element_type=f32
        )
        for c_ref, w_ref in zip(cots, weights)
    )
    grad_query_ref[...] = (grad_in * summed_ref[...].astype(f32)).astype(bf16)
    grad_conv_ref[...] = (grad_in * q_ref[...].astype(f32)).astype(bf16)
    for lanes, rows in groups_of(q_ref, rates_ref):
        put_segments(u_ref, grad_conv_ref[:, lanes].astype(f32))
        local_ends(u_ref, rates_ref[rows], ends_ref, starts_ref, lanes, rows, True)


def backward_kernel(
    g_ref, k_ref, v_ref, rates_ref, amp_ref, skip_ref, starts_ref, init_ref, *refs
):
    *part_refs, grad_key_ref, grad_value_ref, mixed_ref, u_ref, y_ref = refs
    mixed_ref[...] = sum(part_ref[...].astype(f32) for part_ref in part_refs).astype(bf16)
    for lanes, rows in groups_of(k_ref, rates_ref):
        put_segments(u_ref, g_ref[:, lanes].astype(f32))
        full_scan(
            u_ref, y_ref, rates_ref[rows], amp_ref[rows], starts_ref,
            init_ref[rows], lanes, True,
        )
        back = get_segments(y_ref).astype(bf16).astype(f32)
        grad = back + skip_ref[:, lanes] * get_segments(u_ref)
        grad_key_ref[:, lanes] = (grad * v_ref[:, lanes].astype(f32)).astype(bf16)
        grad_value_ref[:, lanes] = (grad * k_ref[:, lanes].astype(f32)).astype(bf16)


def exchange_kernel(
    length, flipped, ends_ref, rates_ref, init_ref,
    mine_ref, before_ref, back_ref, send_out, recv_out, send_back, recv_back,
):
    count = ends_ref.shape[0]
    me, row = lax.axis_index("ctx"), lax.axis_index("tp")
    partners = [lax.rem(me + p, count) for p in range(1, count)]

    barrier = pltpu.get_barrier_semaphore()
    for to in partners:
        pl.semaphore_signal(
            barrier, inc=1, device_id=(to, row), device_id_type=pl.DeviceIdType.MESH
        )
    pl.semaphore_wait(barrier, count - 1)

    def send(src_ref, dst_ref, sent, arrived):
        copies = [
            pltpu.make_async_remote_copy(
                src_ref=src_ref.at[to],
                dst_ref=dst_ref.at[me],
                send_sem=sent.at[p],
                recv_sem=arrived.at[p],
                device_id=(to, row),
                device_id_type=pl.DeviceIdType.MESH,
            )
            for p, to in enumerate(partners)
        ]
        for copy in copies:
            copy.start()
        return copies

    outward = send(ends_ref, mine_ref, send_out, recv_out)
    mine_ref[me] = ends_ref[me]
    factor = jnp.exp(-rates_ref[me] * float(length))
    for copy in outward:
        copy.wait_recv()
    state = jnp.zeros_like(factor)
    for place in reversed(range(count)) if flipped else range(count):
        before_ref[place] = state
        state = factor * state + mine_ref[place]
    homeward = send(before_ref, back_ref, send_back, recv_back)
    back_ref[me] = before_ref[me]
    for copy in homeward:
        copy.wait_recv()
    init_ref[...] = back_ref[...]
    for copy in outward + homeward:
        copy.wait_send()


def across_devices(ends, rates, length, flipped):
    count = lax.axis_size("ctx")
    rows = ends.shape[0]
    shape = (count, rows // count, LANES)
    whole = pl.BlockSpec(memory_space=pltpu.VMEM)
    init = pl.pallas_call(
        functools.partial(exchange_kernel, length, flipped),
        out_shape=jax.ShapeDtypeStruct(shape, f32),
        in_specs=[whole, whole],
        out_specs=whole,
        scratch_shapes=[pltpu.VMEM(shape, f32)] * 3
        + [pltpu.SemaphoreType.DMA((count - 1,))] * 4,
        compiler_params=pltpu.CompilerParams(
            collective_id=1 if flipped else 0, has_side_effects=True
        ),
        cost_estimate=LIGHT,
        name="exchange_back" if flipped else "exchange_forward",
    )(ends.reshape(shape), rates.reshape(shape))
    return init.reshape(rows, LANES)


def per_device(q, k, v, cot, weight, decay_rates, residues, skip_gain):
    length, channels = q.shape
    modes = decay_rates.shape[1]
    n_tp = lax.axis_size("tp")
    me = lax.axis_index("tp").astype(jnp.int32)
    shared = cot.shape[1]

    others = [
        lax.ppermute(cot, "tp", [((i + s) % n_tp, i) for i in range(n_tp)])
        for s in range(1, n_tp)
    ]

    def by_group(x):
        x = jnp.transpose(x.reshape(channels // LANES, LANES, modes), (0, 2, 1))
        return x.reshape(channels // LANES * modes, LANES)

    rates = by_group(decay_rates)
    amp = by_group(residues * jnp.sqrt(-jnp.expm1(-2.0 * decay_rates)))
    skip = skip_gain.reshape(1, channels)

    block = 256
    steps = channels // block
    wide = pl.BlockSpec((length, block), lambda i: (0, i))
    table = pl.BlockSpec((block // LANES * modes, LANES), lambda i: (i, 0))
    starts_spec = pl.BlockSpec((modes * SEGS, block), lambda i: (0, i))
    line = pl.BlockSpec((1, block), lambda i: (0, i))
    params = pltpu.CompilerParams(vmem_limit_bytes=LIMIT)
    signal = jax.ShapeDtypeStruct((length, channels), bf16)
    ends_shape = jax.ShapeDtypeStruct((channels // LANES * modes, LANES), f32)
    starts_shape = jax.ShapeDtypeStruct((modes * SEGS, channels), f32)
    scratch = pltpu.VMEM((length + SEGS * GAP, LANES), f32)

    ends, starts = pl.pallas_call(
        forward_ends_kernel,
        grid=(steps,),
        in_specs=[wide, wide, table],
        out_specs=[table, starts_spec],
        out_shape=[ends_shape, starts_shape],
        scratch_shapes=[scratch],
        compiler_params=params,
        cost_estimate=LIGHT,
        name="forward_ends",
    )(k, v, rates)
    init = across_devices(ends, rates, length, False)
    output_in, summed = pl.pallas_call(
        forward_kernel,
        grid=(steps,),
        in_specs=[wide, wide, wide, table, table, line, starts_spec, table],
        out_specs=[wide, wide],
        out_shape=[signal, signal],
        scratch_shapes=[scratch, scratch],
        compiler_params=params,
        cost_estimate=LIGHT,
        name="forward_scan",
    )(q, k, v, rates, amp, skip, starts, init)

    cols = 512
    per_target = shared // cols

    def project(target):
        return pl.pallas_call(
            matmul_kernel,
            grid_spec=pltpu.PrefetchScalarGridSpec(
                num_scalar_prefetch=1,
                grid=(per_target,),
                in_specs=[
                    pl.BlockSpec((length, channels), lambda i, at: (0, 0)),
                    pl.BlockSpec((channels, cols), lambda i, at: (0, at[0] * per_target + i)),
                ],
                out_specs=pl.BlockSpec((length, cols), lambda i, at: (0, i)),
            ),
            out_shape=jax.ShapeDtypeStruct((length, shared), bf16),
            compiler_params=params,
            cost_estimate=LIGHT,
            name="project",
        )(target.reshape(1), output_in, weight)

    parts = [project(lax.rem(me + s, n_tp)) for s in range(1, n_tp)]
    others, parts = lax.optimization_barrier((others, parts))
    received = [
        lax.ppermute(part, "tp", [(i, (i + s) % n_tp) for i in range(n_tp)])
        for s, part in enumerate(parts, 1)
    ]

    def weight_spec(s):
        return pl.BlockSpec((block, shared), lambda i, at: (i, lax.rem(at[0] + s, n_tp)))

    def with_at(spec):
        return pl.BlockSpec(spec.block_shape, lambda i, at: spec.index_map(i))

    grad_query, grad_conv, back_ends, back_starts = pl.pallas_call(
        functools.partial(grad_kernel, n_tp),
        grid_spec=pltpu.PrefetchScalarGridSpec(
            num_scalar_prefetch=1,
            grid=(steps,),
            in_specs=[pl.BlockSpec((length, shared), lambda i, at: (0, 0))] * n_tp
            + [weight_spec(s) for s in range(n_tp)]
            + [with_at(wide), with_at(wide), with_at(table)],
            out_specs=[with_at(wide), with_at(wide), with_at(table), with_at(starts_spec)],
            scratch_shapes=[scratch],
        ),
        out_shape=[signal, signal, ends_shape, starts_shape],
        compiler_params=params,
        cost_estimate=LIGHT,
        name="grad_projection",
    )(me.reshape(1), cot, *others, *([weight] * n_tp), q, summed, rates)
    own = project(me)
    back_init = across_devices(back_ends, rates, length, True)
    grad_key, grad_value, mixed = pl.pallas_call(
        backward_kernel,
        grid=(steps,),
        in_specs=[wide, wide, wide, table, table, line, starts_spec, table]
        + [wide] * n_tp,
        out_specs=[wide, wide, wide],
        out_shape=[signal, signal, signal],
        scratch_shapes=[scratch, scratch],
        compiler_params=params,
        cost_estimate=LIGHT,
        name="backward_scan",
    )(grad_conv, k, v, rates, amp, skip, back_starts, back_init, own, *received)

    return (mixed, grad_query, grad_key, grad_value)


def solution(mesh):
    spread = P("ctx", "tp")
    by_tp = P("tp", None)
    return jax.shard_map(
        per_device,
        mesh=mesh,
        in_specs=(spread, spread, spread, spread, by_tp, by_tp, by_tp, P("tp")),
        out_specs=(spread, spread, spread, spread),
        check_vma=False,
    )
```
